256 devices in a mesh: dp: 16 (over x, z_lo), tensor: 16 (over y, z_hi, core).
Axes of the slice: x: 4, y: 4, z: 8 (z_hi: 2, z_lo: 4; z = z_hi * 4 + z_lo), core: 2. Of those that a mesh axis runs over, the one named last changes fastest.
Arguments:
- tokens: bfloat16 [4096, 4096], P('dp'), may hold values from -6 to 6
- in_weight: bfloat16 [4096, 18560], P('dp', 'tensor'), may hold values from -0.09375 to 0.09375
- out_weight: bfloat16 [4096, 8192], P('dp', 'tensor'), may hold values from -0.0625 to 0.0625
- a_log: float32 [128], P('tensor'), may hold values from -4 to 1.5
- dt_bias: float32 [128], P('tensor'), may hold values from -4 to -1
- d_skip: float32 [128], P('tensor'), may hold values from 0.5 to 1.5
- norm_gain: float32 [8192], P('tensor'), may hold values from 0.1 to 1.9
- d_mixed: bfloat16 [4096, 4096], P('dp'), may hold values from -0.09375 to 0.09375
Outputs:
- mixed: bfloat16 [4096, 4096], P('dp', 'tensor')
- grad_in_weight: float32 [4096, 18560], P('dp', 'tensor')
- grad_out_weight: float32 [4096, 8192], P('dp', 'tensor')
- grad_a_log: float32 [128], P('tensor')
- grad_dt_bias: float32 [128], P('tensor')
- grad_d_skip: float32 [128], P('tensor')
- grad_norm_gain: float32 [8192], P('tensor')
The draws below stay inside these ranges and needn't reach their ends.
All inputs are finite; a program needn't handle non-finite values.
Results may differ from the reference program's by a relative error of at most 0.03.
Values may be sent and summed in bfloat16 or wider, within the bound.
No kernel may reach another device: no remote copies, remote signals or barrier semaphores. Data moves between devices by JAX's collectives and lax.ppermute only.
A program may use at most 128 MiB of HBM per device.

```python
import jax
import jax.numpy as jnp
from jax import lax

D = 4096
HEADS_DEV = 8
HEAD_DIM = 64
N_STATE = 128
TOK_DEV = 256
INNER_DEV = 512
PROJ_DEV = 1160
HEADS = 128
INNER = 8192
TOKENS = 4096
N_DP = 16
N_TENSOR = 16


def steps_of(own_key, extent, split, low, largest):
    loudness, own = 1.0, jax.random.fold_in(own_key, 6)
    for position, shards_of in split:
        steps = jnp.exp(jax.random.uniform(jax.random.fold_in(own, position), (shards_of,), jnp.float32, low / len(split), largest / len(split)))
        loudness = loudness * jnp.repeat(steps, extent[position] // shards_of).reshape([-1 if axis == position else 1 for axis in range(len(extent))])
    return loudness


def gaussian(own_key, dims, scale, reach, cuts=(), held_as=jnp.bfloat16):
    array = scale * jax.random.normal(own_key, dims, jnp.float32)
    if cuts:
        array = array * steps_of(own_key, dims, cuts, -0.22, 0.18)
    return jnp.clip(array, -reach, reach).astype(held_as)


def setup_inputs(seed: int = 0) -> dict:
    key_list = jax.random.split(jax.random.key(seed), 9)
    return {
        "tokens": gaussian(key_list[0], (TOKENS, D), 1.0, 6.0, ((0, 16),)),
        "in_weight": gaussian(key_list[1], (D, PROJ_DEV * N_TENSOR), D ** -0.5, 0.09375, ((0, 16), (1, 16))),
        "out_weight": gaussian(key_list[2], (D, INNER), INNER ** -0.5, 0.0625, ((0, 16), (1, 16))),
        "a_log": jnp.clip(-4.0 + 5.5 * jax.random.uniform(key_list[3], (HEADS,), jnp.float32) ** steps_of(key_list[3], (HEADS,), ((0, 16),), -0.2, 0.2), -4.0, 1.5),
        "dt_bias": jnp.clip(-4.0 + 3.0 * jax.random.uniform(key_list[4], (HEADS,), jnp.float32) ** steps_of(key_list[4], (HEADS,), ((0, 16),), -0.2, 0.2), -4.0, -1.0),
        "d_skip": jnp.clip(0.5 + 1.0 * jax.random.uniform(key_list[5], (HEADS,), jnp.float32) ** steps_of(key_list[5], (HEADS,), ((0, 16),), -0.2, 0.2), 0.5, 1.5),
        "norm_gain": jnp.clip(1.0 + 0.18 * jax.random.normal(key_list[6], (INNER,), jnp.float32), 0.1, 1.9),
        "d_mixed": gaussian(key_list[7], (TOKENS, D), (1.0 / (TOK_DEV * N_DP) ** 0.5), 0.09375, ((0, 16),)),
    }


eps = 1e-05

def mixer_part(projected, partner_bc, a_log, dt_bias, d_skip, lower_half):
    heads = a_log.shape[0]
    inner_width = heads * HEAD_DIM
    half_state = partner_bc.shape[1] // 2
    seq_len = projected.shape[0]
    gate_part = projected[:, :inner_width]
    inputs = projected[:, inner_width:2 * inner_width].reshape(seq_len, heads, HEAD_DIM)
    base = 2 * inner_width
    own_b = projected[:, base:base + half_state]
    own_c = projected[:, base + half_state:base + 2 * half_state]
    step_raw = projected[:, base + 2 * half_state:]
    other_b = partner_bc[:, :half_state]
    other_c = partner_bc[:, half_state:]
    full_b = jnp.where(lower_half, jnp.concatenate([own_b, other_b], 1), jnp.concatenate([other_b, own_b], 1))
    full_c = jnp.where(lower_half, jnp.concatenate([own_c, other_c], 1), jnp.concatenate([other_c, own_c], 1))
    step_size = jax.nn.softplus(step_raw + dt_bias)
    log_decay = jnp.cumsum(step_size * -jnp.exp(a_log), axis=0)
    causal = (jnp.arange(seq_len)[:, None] >= jnp.arange(seq_len)[None, :])[:, :, None]
    log_ratio = log_decay[:, None, :] - log_decay[None, :, :]
    decay = jnp.where(causal, jnp.exp(jnp.where(causal, log_ratio, 0.0)), 0.0)
    affinity = jnp.dot(full_c.astype(jnp.bfloat16), full_b.T.astype(jnp.bfloat16), preferred_element_type=jnp.float32)
    weights_ts = decay * affinity[:, :, None] * step_size[None, :, :]
    outputs = jnp.einsum('tsh,shp->thp', weights_ts, inputs, precision=lax.Precision.HIGHEST)
    outputs = outputs + d_skip[None, :, None] * inputs
    gated = outputs.reshape(seq_len, inner_width) * jax.nn.silu(gate_part)
    return (gated, lax.optimization_barrier(jnp.sum(gated * gated, axis=1)))

def sequence_forward(projected, a_log, dt_bias, d_skip, norm_gain):
    partner_index = jnp.arange(N_TENSOR) ^ 1
    lower_half = jnp.arange(N_TENSOR) % 2 == 0
    base = 2 * INNER_DEV
    state_cols = projected[:, :, base:base + N_STATE]
    partner_bc = state_cols[:, partner_index, :]
    gated, squares = jax.vmap(mixer_part, in_axes=(1, 1, 0, 0, 0, 0))(projected, partner_bc, a_log, dt_bias, d_skip, lower_half)
    total_sq = squares + squares[partner_index]
    scale_rows = lax.rsqrt(total_sq / (2 * INNER_DEV) + eps)
    return gated * scale_rows[:, :, None] * norm_gain[:, None, :]

def reference(tokens, in_weight, out_weight, a_log, dt_bias, d_skip, norm_gain, d_mixed):
    projected = jnp.dot(tokens, in_weight, preferred_element_type=jnp.float32).astype(jnp.bfloat16)
    proj_seq = projected.reshape(N_DP, TOK_DEV, N_TENSOR, PROJ_DEV)
    token_seq = tokens.reshape(N_DP, TOK_DEV, D)
    cot_seq = d_mixed.reshape(N_DP, TOK_DEV, D)
    a_two = a_log.reshape(N_TENSOR, HEADS_DEV)
    bias_two = dt_bias.reshape(N_TENSOR, HEADS_DEV)
    skip_two = d_skip.reshape(N_TENSOR, HEADS_DEV)
    gain_two = norm_gain.reshape(N_TENSOR, INNER_DEV)
    out_f32 = out_weight.astype(jnp.float32)
    out_blocks = out_f32.reshape(D, N_TENSOR, INNER_DEV)

    def step_fn(carry, items):
        proj_block, token_block, cot_block = items
        proj_f32 = proj_block.astype(jnp.float32)
        normed_f32, pull_back = jax.vjp(sequence_forward, proj_f32, a_two, bias_two, skip_two, gain_two)
        normed = normed_f32.astype(jnp.bfloat16)
        parts = jnp.einsum('tli,dti->tld', normed.astype(jnp.float32), out_blocks, precision=lax.Precision.HIGHEST)
        parts = lax.optimization_barrier(parts.astype(jnp.bfloat16)).astype(jnp.float32)
        mixed_seq = lax.optimization_barrier(jnp.sum(parts, axis=0)).astype(jnp.bfloat16)
        cot_f32 = cot_block.astype(jnp.float32)
        d_normed = jnp.dot(cot_f32, out_f32, precision=lax.Precision.HIGHEST)
        d_normed = d_normed.reshape(TOK_DEV, N_TENSOR, INNER_DEV).transpose(1, 0, 2)
        d_proj, d_a, d_bias, d_skip_g, d_gain = pull_back(d_normed)
        d_proj = d_proj.astype(jnp.bfloat16).reshape(TOK_DEV, N_TENSOR * PROJ_DEV)
        in_term = jnp.dot(token_block.T, d_proj, preferred_element_type=jnp.float32)
        in_term = lax.optimization_barrier(in_term.astype(jnp.bfloat16)).astype(jnp.float32)
        normed_flat = normed.transpose(1, 0, 2).reshape(TOK_DEV, N_TENSOR * INNER_DEV)
        out_term = jnp.dot(cot_block.T, normed_flat, preferred_element_type=jnp.float32)
        out_term = lax.optimization_barrier(out_term.astype(jnp.bfloat16)).astype(jnp.float32)
        grad_in, grad_out, grad_a, grad_bias, grad_skip, grad_gain = carry
        carry = (grad_in + in_term, grad_out + out_term, grad_a + d_a, grad_bias + d_bias, grad_skip + d_skip_g, grad_gain + d_gain)
        return (carry, mixed_seq)
    start_carry = (jnp.zeros((D, N_TENSOR * PROJ_DEV), jnp.float32), jnp.zeros((D, N_TENSOR * INNER_DEV), jnp.float32), jnp.zeros((N_TENSOR, HEADS_DEV), jnp.float32), jnp.zeros((N_TENSOR, HEADS_DEV), jnp.float32), jnp.zeros((N_TENSOR, HEADS_DEV), jnp.float32), jnp.zeros((N_TENSOR, INNER_DEV), jnp.float32))
    final_carry, mixed_all = lax.scan(step_fn, start_carry, (proj_seq, token_seq, cot_seq))
    grad_in, grad_out, grad_a, grad_bias, grad_skip, grad_gain = final_carry
    mixed = mixed_all.reshape(N_DP * TOK_DEV, D)
    return (mixed, grad_in, grad_out, grad_a.reshape(-1), grad_bias.reshape(-1), grad_skip.reshape(-1), grad_gain.reshape(-1))
```

```python
import jax
import jax.numpy as jnp
from jax import lax
from jax.sharding import PartitionSpec as P

HEAD_DIM = 64
N_STATE = 128
N_X = 4
N_Z = 4

eps = 1e-05

CORE = [(i, i ^ 1) for i in range(16)]
Z_HI = [(i, i ^ 2) for i in range(16)]


def along_x(shift):
    return [(x * 4 + z, (x + shift) % 4 * 4 + z) for x in range(4) for z in range(4)]


def along_z(pairs):
    return [(x * 4 + a, x * 4 + b) for x in range(4) for a, b in pairs]


Z_NEAR = along_z([(0, 1), (1, 0), (2, 3), (3, 2)])
Z_MID = along_z([(1, 2), (2, 1)])
Z_OUTWARD = along_z([(1, 0), (2, 3)])
Z_INWARD = along_z([(0, 1), (3, 2)])


def turned(turn):
    route = []
    for x in range(4):
        for z in range(4):
            for y in range(4):
                for r in range(4):
                    source = (x * 4 + z) * 16 + y * 4 + r
                    target = ((y + turn) % 4 * 4 + z) * 16 + x * 4 + r
                    route.append((source, target))
    return route


def after(value, *others):
    return lax.optimization_barrier((value,) + others)[0]


def mixer_part(projected, partner_bc, a_log, dt_bias, d_skip, lower_half):
    heads = a_log.shape[0]
    inner_width = heads * HEAD_DIM
    half_state = partner_bc.shape[1] // 2
    seq_len = projected.shape[0]
    inputs = projected[:, :inner_width].reshape(seq_len, heads, HEAD_DIM)
    base = inner_width
    own_b = projected[:, base : base + half_state]
    own_c = projected[:, base + half_state : base + 2 * half_state]
    step_raw = projected[:, base + 2 * half_state :]
    other_b = partner_bc[:, :half_state]
    other_c = partner_bc[:, half_state:]
    full_b = jnp.where(
        lower_half, jnp.concatenate([own_b, other_b], 1), jnp.concatenate([other_b, own_b], 1)
    )
    full_c = jnp.where(
        lower_half, jnp.concatenate([own_c, other_c], 1), jnp.concatenate([other_c, own_c], 1)
    )
    step_size = jax.nn.softplus(step_raw + dt_bias)
    log_decay = jnp.cumsum(step_size * -jnp.exp(a_log), axis=0)
    causal = (jnp.arange(seq_len)[:, None] >= jnp.arange(seq_len)[None, :])[:, :, None]
    log_ratio = log_decay[:, None, :] - log_decay[None, :, :]
    decay = jnp.where(causal, jnp.exp(jnp.where(causal, log_ratio, 0.0)), 0.0)
    affinity = jnp.dot(
        full_c.astype(jnp.bfloat16),
        full_b.T.astype(jnp.bfloat16),
        preferred_element_type=jnp.float32,
    )
    weights_ts = decay * affinity[:, :, None] * step_size[None, :, :]
    outputs = jnp.einsum("tsh,shp->thp", weights_ts, inputs, precision=lax.Precision.HIGHEST)
    outputs = outputs + d_skip[None, :, None] * inputs
    return outputs.reshape(seq_len, inner_width)


def gate_part(outputs, gate):
    gated = outputs * jax.nn.silu(gate)
    return (gated, jnp.sum(gated * gated, axis=1))


def gather_z(block, is_mid):
    near = lax.ppermute(block, "dp", Z_NEAR)
    mid_own = lax.ppermute(block, "dp", Z_MID)
    mid_near = lax.ppermute(near, "dp", Z_MID)
    out_own = lax.ppermute(mid_own, "dp", Z_OUTWARD)
    out_near = lax.ppermute(mid_near, "dp", Z_OUTWARD)
    third = jnp.where(is_mid, mid_own, out_own)
    fourth = jnp.where(is_mid, mid_near, out_near)
    return jnp.concatenate([block, near, third, fourth], 0), mid_near


def scatter_z(part):
    fourth = part(3)
    in_fourth = lax.ppermute(fourth.astype(jnp.bfloat16), "dp", Z_INWARD)
    third = part(2)
    in_third = lax.ppermute(third.astype(jnp.bfloat16), "dp", Z_INWARD)
    mid_near = lax.ppermute(
        (fourth + in_fourth.astype(jnp.float32)).astype(jnp.bfloat16), "dp", Z_MID
    )
    mid_own = lax.ppermute(
        (third + in_third.astype(jnp.float32)).astype(jnp.bfloat16), "dp", Z_MID
    )
    near = lax.ppermute(
        (part(1) + mid_near.astype(jnp.float32)).astype(jnp.bfloat16), "dp", Z_NEAR
    )
    return part(0) + near.astype(jnp.float32) + mid_own.astype(jnp.float32)


def gather_x(block):
    before = lax.ppermute(block, "dp", along_x(1))
    behind = lax.ppermute(block, "dp", along_x(3))
    far = lax.ppermute(block, "dp", along_x(2))
    return jnp.concatenate([block, before, far, behind], 0)


def scatter_x(part):
    far = lax.ppermute(part(2).astype(jnp.bfloat16), "dp", along_x(2))
    before = lax.ppermute(part(1).astype(jnp.bfloat16), "dp", along_x(3))
    behind = lax.ppermute(part(3).astype(jnp.bfloat16), "dp", along_x(1))
    return (
        part(0)
        + far.astype(jnp.float32)
        + before.astype(jnp.float32)
        + behind.astype(jnp.float32)
    )


def per_device(tokens, in_weight, out_weight, a_log, dt_bias, d_skip, norm_gain, d_mixed):
    inner_width = norm_gain.shape[0]
    seq_len = tokens.shape[0]
    half = seq_len // 2
    blk = in_weight.shape[0]
    dp = lax.axis_index("dp")
    tensor = lax.axis_index("tensor")
    x, z = dp // N_Z, dp % N_Z
    y, z_hi, core = tensor // 4, tensor // 2 % 2, tensor % 2
    low = z < 2
    is_mid = (z == 1) | (z == 2)
    lower_half = core == 0
    slots = [z, z ^ 1, jnp.where(low, 2, 1), jnp.where(low, 3, 0)]

    def dot(a, b, dims):
        return lax.dot_general(a, b, (dims, ((), ())), preferred_element_type=jnp.float32)

    def half_first(a):
        return jnp.where(lower_half, a, jnp.concatenate([a[half:], a[:half]], 0))

    def regroup(a):
        def slab(shift, start):
            base = (x + shift) % N_X * (N_Z * blk)
            return jnp.concatenate(
                [lax.dynamic_slice(a, (start, base + s * blk), (half, blk)) for s in slots], 1
            )

        mine, other = core * half, half - core * half
        received = [
            lax.ppermute(slab(1, mine), "dp", along_x(1)),
            lax.ppermute(slab(2, mine), "dp", along_x(2)),
            lax.ppermute(slab(3, mine), "dp", along_x(3)),
        ]
        rows = [slab(0, mine), slab(0, other)]
        for r in received:
            rows += [r, lax.ppermute(r, "tensor", CORE)]
        return jnp.concatenate(rows, 0), received[0]

    def row_slot(a, s):
        return a[s * seq_len : (s + 1) * seq_len]

    def col_slot(a, s):
        return a[:, s * blk : (s + 1) * blk]

    w_scan, scan_done = gather_z(in_weight[:, inner_width:], is_mid)
    tok, tok_done = regroup(tokens)
    w_gate, gate_done = gather_z(after(in_weight[:, :inner_width], scan_done), is_mid)
    cot, _ = regroup(after(d_mixed, tok_done))
    w_out, _ = gather_z(after(out_weight, gate_done), is_mid)

    def project(weight):
        share = scatter_x(lambda s: dot(row_slot(tok, s), weight, ((1,), (0,))))
        return half_first(share.astype(jnp.bfloat16))

    proj_scan = project(w_scan)
    own_bc = proj_scan[:, inner_width : inner_width + N_STATE]
    partner_bc = lax.ppermute(own_bc, "tensor", CORE)

    def section_scan(proj_vals, partner_vals, rates, biases, skips):
        return mixer_part(proj_vals, partner_vals, rates, biases, skips, lower_half)

    outputs, pull_scan = jax.vjp(
        section_scan,
        proj_scan.astype(jnp.float32),
        partner_bc.astype(jnp.float32),
        a_log,
        dt_bias,
        d_skip,
    )
    proj_gate = project(w_gate)
    (gated, squares), pull_gate = jax.vjp(gate_part, outputs, proj_gate.astype(jnp.float32))
    total_sq = squares + lax.ppermute(squares, "tensor", CORE)

    def section_norm(gated_vals, sums, gains):
        return gated_vals * lax.rsqrt(sums / (2 * inner_width) + eps)[:, None] * gains

    normed_f32, pull_norm = jax.vjp(section_norm, gated, total_sq, norm_gain)
    d_normed = half_first(
        scatter_x(lambda s: dot(row_slot(cot, s), w_out, ((1,), (0,))))
    )
    d_gated, d_total, d_gain = pull_norm(d_normed)
    d_squares = d_total + lax.ppermute(d_total, "tensor", CORE)
    d_outputs, d_gate = pull_gate((d_gated, d_squares))

    normed = gather_x(half_first(normed_f32.astype(jnp.bfloat16)))
    grad_out = scatter_z(lambda s: dot(col_slot(cot, s), normed, ((0,), (0,))))

    gate_all = gather_x(half_first(d_gate.astype(jnp.bfloat16)))
    grad_gate = scatter_z(lambda s: dot(col_slot(tok, s), gate_all, ((0,), (0,))))

    d_scan, d_partner, d_rates, d_biases, d_skips = pull_scan(d_outputs)
    returned = lax.ppermute(d_partner.astype(jnp.bfloat16), "tensor", CORE)
    d_scan = jnp.concatenate(
        [
            d_scan[:, :inner_width],
            d_scan[:, inner_width : inner_width + N_STATE] + returned.astype(jnp.float32),
            d_scan[:, inner_width + N_STATE :],
        ],
        1,
    )
    scan_all = gather_x(half_first(d_scan.astype(jnp.bfloat16)))
    grad_scan = scatter_z(lambda s: dot(col_slot(tok, s), scan_all, ((0,), (0,))))
    grad_in = jnp.concatenate([grad_gate, grad_scan], 1)

    shares = dot(normed, w_out, ((1,), (1,))).reshape(N_X, 2, half, N_Z * blk)
    passed = lax.ppermute(shares[:, 1].astype(jnp.bfloat16), "tensor", CORE)
    chip = (shares[:, 0] + passed.astype(jnp.float32)).astype(jnp.bfloat16)
    summed = 0.0
    for turn in range(4):
        slot = (x - y - turn) % 4
        piece = lax.dynamic_index_in_dim(chip, slot, 0, keepdims=False)
        summed += lax.ppermute(piece, ("dp", "tensor"), turned(turn)).astype(jnp.float32)
    summed = summed.reshape(half, 2, 2 * blk)
    keep = z_hi ^ jnp.where(low, 0, 1)
    sent = lax.dynamic_index_in_dim(summed, 1 - keep, 1, keepdims=False)
    kept = lax.dynamic_index_in_dim(summed, keep, 1, keepdims=False)
    kept = kept + lax.ppermute(sent.astype(jnp.bfloat16), "tensor", Z_HI).astype(jnp.float32)
    first = jnp.where(keep == 0, slots[0], slots[2]) % 2
    kept = kept.astype(jnp.bfloat16).reshape(half, 2, blk)
    at = core ^ first
    mine = lax.dynamic_index_in_dim(kept, at, 1, keepdims=False)
    theirs = lax.dynamic_index_in_dim(kept, 1 - at, 1, keepdims=False)
    mixed = half_first(jnp.concatenate([mine, lax.ppermute(theirs, "tensor", CORE)], 0))

    small = jnp.concatenate([d_rates, d_biases, d_skips, d_gain])
    for bit in range(4):
        small = small + lax.ppermute(small, "dp", [(i, i ^ 1 << bit) for i in range(16)])
    heads = a_log.shape[0]
    return (
        mixed,
        grad_in,
        grad_out,
        small[:heads],
        small[heads : 2 * heads],
        small[2 * heads : 3 * heads],
        small[3 * heads :],
    )


def solution(mesh):
    return jax.shard_map(
        per_device,
        mesh=mesh,
        in_specs=(
            P("dp", None),
            P("dp", "tensor"),
            P("dp", "tensor"),
            P("tensor"),
            P("tensor"),
            P("tensor"),
            P("tensor"),
            P("dp", None),
        ),
        out_specs=(
            P("dp", "tensor"),
            P("dp", "tensor"),
            P("dp", "tensor"),
            P("tensor"),
            P("tensor"),
            P("tensor"),
            P("tensor"),
        ),
        check_vma=False,
    )
```

```python
import jax
import jax.numpy as jnp
from jax import lax
from jax.sharding import PartitionSpec as P

HEAD_DIM = 64
N_STATE = 128
N_X = 4
N_Z = 4

eps = 1e-05

CORE = [(i, i ^ 1) for i in range(16)]
Z_HI = [(i, i ^ 2) for i in range(16)]


TRANSPOSED = [
    ((x * 4 + z) * 16 + y * 4 + r, (y * 4 + z) * 16 + x * 4 + r)
    for x in range(4)
    for z in range(4)
    for y in range(4)
    for r in range(4)
]


def mixer_part(projected, partner_bc, a_log, dt_bias, d_skip, lower_half):
    heads = a_log.shape[0]
    inner_width = heads * HEAD_DIM
    half_state = partner_bc.shape[1] // 2
    seq_len = projected.shape[0]
    inputs = projected[:, :inner_width].reshape(seq_len, heads, HEAD_DIM)
    base = inner_width
    own_b = projected[:, base : base + half_state]
    own_c = projected[:, base + half_state : base + 2 * half_state]
    step_raw = projected[:, base + 2 * half_state :]
    other_b = partner_bc[:, :half_state]
    other_c = partner_bc[:, half_state:]
    full_b = jnp.where(
        lower_half, jnp.concatenate([own_b, other_b], 1), jnp.concatenate([other_b, own_b], 1)
    )
    full_c = jnp.where(
        lower_half, jnp.concatenate([own_c, other_c], 1), jnp.concatenate([other_c, own_c], 1)
    )
    step_size = jax.nn.softplus(step_raw + dt_bias)
    log_decay = jnp.cumsum(step_size * -jnp.exp(a_log), axis=0)
    causal = (jnp.arange(seq_len)[:, None] >= jnp.arange(seq_len)[None, :])[:, :, None]
    log_ratio = log_decay[:, None, :] - log_decay[None, :, :]
    decay = jnp.where(causal, jnp.exp(jnp.where(causal, log_ratio, 0.0)), 0.0)
    affinity = jnp.dot(
        full_c.astype(jnp.bfloat16),
        full_b.T.astype(jnp.bfloat16),
        preferred_element_type=jnp.float32,
    )
    weights_ts = decay * affinity[:, :, None] * step_size[None, :, :]
    outputs = jnp.einsum("tsh,shp->thp", weights_ts, inputs, precision=lax.Precision.HIGHEST)
    outputs = outputs + d_skip[None, :, None] * inputs
    return outputs.reshape(seq_len, inner_width)


def gate_part(outputs, gate):
    gated = outputs * jax.nn.silu(gate)
    return (gated, jnp.sum(gated * gated, axis=1))


def together(*values):
    return lax.optimization_barrier(values)


def send_x(block, step):
    return lax.ppermute(block, "dp", [(i, i ^ step * N_Z) for i in range(16)])


def send_z(block, step):
    return lax.ppermute(block, "dp", [(i, i ^ step) for i in range(16)])


def send_y(block, step):
    return lax.ppermute(block, "tensor", [(i, i ^ step * 4) for i in range(16)])


def swap_core(block):
    return lax.ppermute(block, "tensor", CORE)


def f32(a):
    return a.astype(jnp.float32)


def bf16(a):
    return a.astype(jnp.bfloat16)


def per_device(tokens, in_weight, out_weight, a_log, dt_bias, d_skip, norm_gain, d_mixed):
    inner_width = norm_gain.shape[0]
    seq_len = tokens.shape[0]
    half = seq_len // 2
    blk = in_weight.shape[0]
    wide = N_Z * blk
    dp = lax.axis_index("dp")
    tensor = lax.axis_index("tensor")
    x, z = dp // N_Z, dp % N_Z
    y, z_hi, core = tensor // 4, tensor // 2 % 2, tensor % 2
    lower_half = core == 0
    mine, other = core * half, half - core * half


    def dot(a, b, dims):
        return lax.dot_general(a, b, (dims, ((), ())), preferred_element_type=jnp.float32)

    def half_first(a):
        return jnp.where(lower_half, a, jnp.concatenate([a[half:], a[:half]], 0))

    def slab(a, shift, start):
        return lax.dynamic_slice(a, (start, (x ^ shift) * wide), (half, wide))

    def grouped(a, received):
        rows = [slab(a, 0, mine), slab(a, 0, other)]
        for r in received:
            rows += r
        return lax.optimization_barrier(jnp.concatenate(rows, 0))

    def by_slot(a):
        columns = [lax.dynamic_slice(a, (0, (z ^ s) * blk), (a.shape[0], blk)) for s in range(N_Z)]
        return lax.optimization_barrier(jnp.concatenate(columns, 1))

    def rows_of(own, received):
        return lax.optimization_barrier(jnp.concatenate([own, *received], 0))

    def slot(a, s, size):
        return a[s * size : (s + 1) * size]

    def cols_of(own, received):
        return lax.optimization_barrier(jnp.concatenate([own, *received], 1))

    def col_slot(a, s, size):
        return a[:, s * size : (s + 1) * size]

    def gather_x(block):
        return [send_x(block, s) for s in (1, 2, 3)]

    def to_z(share, step):
        return send_z(slot(share, step, blk), step)

    def to_z_cols(share, step):
        return send_z(col_slot(share, step, blk), step)

    def total(own, received):
        return f32(own) + sum(f32(r) for r in received)

    in_t = in_weight.T
    in_2 = send_z(in_t, 2)
    tok_in = [send_x(slab(tokens, s, mine), s) for s in (1, 2, 3)]
    in_t, in_2, tok_in = together(in_t, in_2, tok_in)

    in_3, in_1 = send_z(in_t, 3), send_z(in_t, 1)
    cot_in = [send_x(slab(d_mixed, s, mine), s) for s in (1, 2, 3)]
    tok = by_slot(grouped(tokens, [(r, swap_core(r)) for r in tok_in]))
    in_3, in_1, cot_in, tok, own_out = together(in_3, in_1, cot_in, tok, out_weight)

    share_in = bf16(dot(cols_of(in_t, [in_1, in_2, in_3]), tok, ((1,), (1,))))
    proj_in = [send_x(col_slot(share_in, s, seq_len), s) for s in (1, 2, 3)]
    out_2, out_3, out_1 = [send_z(own_out, s) for s in (2, 3, 1)]
    cot = by_slot(grouped(d_mixed, [(r, swap_core(r)) for r in cot_in]))
    proj_in, out_1, out_2, out_3, own_out, cot = together(
        proj_in, out_1, out_2, out_3, own_out, cot
    )

    w_out = rows_of(own_out, [out_1, out_2, out_3])
    share_cot = bf16(dot(cot, w_out, ((1,), (0,))))
    cot_sums = [send_x(slot(share_cot, s, seq_len), s) for s in (1, 2, 3)]
    projected = half_first(bf16(total(col_slot(share_in, 0, seq_len), proj_in)).T)
    proj_gate = projected[:, :inner_width]
    proj_scan = projected[:, inner_width:]
    own_bc = proj_scan[:, inner_width : inner_width + N_STATE]
    partner_bc = swap_core(own_bc)

    def section_scan(proj_vals, partner_vals, rates, biases, skips):
        return mixer_part(proj_vals, partner_vals, rates, biases, skips, lower_half)

    outputs, pull_scan = jax.vjp(
        section_scan, f32(proj_scan), f32(partner_bc), a_log, dt_bias, d_skip
    )
    (gated, squares), pull_gate = jax.vjp(gate_part, outputs, f32(proj_gate))
    total_sq = squares + swap_core(squares)

    def section_norm(gated_vals, sums, gains):
        return gated_vals * lax.rsqrt(sums / (2 * inner_width) + eps)[:, None] * gains

    normed_f32, pull_norm = jax.vjp(section_norm, gated, total_sq, norm_gain)
    own_normed = half_first(bf16(normed_f32))
    normed_in = gather_x(own_normed)
    cot_sums, normed_in = together(cot_sums, normed_in)

    d_normed = half_first(total(slot(share_cot, 0, seq_len), cot_sums))
    d_gated, d_total, d_gain = pull_norm(d_normed)
    d_squares = d_total + swap_core(d_total)
    d_outputs, d_gate = pull_gate((d_gated, d_squares))
    d_scan, d_partner, d_rates, d_biases, d_skips = pull_scan(d_outputs)
    returned = swap_core(bf16(d_partner))
    d_proj = jnp.concatenate(
        [
            d_gate,
            d_scan[:, :inner_width],
            d_scan[:, inner_width : inner_width + N_STATE] + f32(returned),
            d_scan[:, inner_width + N_STATE :],
        ],
        1,
    )
    own_proj = half_first(bf16(d_proj)).T
    small = jnp.concatenate([d_rates, d_biases, d_skips, d_gain])
    own_proj, small, normed_in = together(own_proj, small, normed_in)

    dproj_in = gather_x(own_proj)
    normed = rows_of(own_normed, normed_in)
    share_out = bf16(dot(cot, normed, ((0,), (0,))))
    out_2, out_3 = to_z(share_out, 2), to_z(share_out, 3)
    shares = bf16(dot(normed, w_out, ((1,), (1,))))

    def halves(first):
        return jnp.concatenate(
            [shares[s * seq_len + first : s * seq_len + first + half] for s in range(N_X)], 0
        )

    chip = bf16(f32(halves(0)) + f32(swap_core(halves(half))))
    small = small + send_z(small, 1)
    dproj_in, out_2, out_3, share_out, chip, small = together(
        dproj_in, out_2, out_3, share_out, chip, small
    )

    share_dproj = bf16(dot(cols_of(own_proj, dproj_in), tok, ((1,), (0,))))

    def piece(step):
        return lax.dynamic_slice(chip, ((x ^ y ^ step) * half, 0), (half, wide))

    y_in = [send_y(piece(step), step) for step in (1, 2, 3)]
    in_2 = to_z_cols(share_dproj, 2)
    out_1 = to_z(share_out, 1)
    summed = total(piece(0), y_in).reshape(half, 2, 2 * blk)
    keep = z_hi ^ z // 2
    sent = bf16(lax.dynamic_index_in_dim(summed, 1 - keep, 1, keepdims=False))
    kept = lax.dynamic_index_in_dim(summed, keep, 1, keepdims=False)
    sent = lax.ppermute(sent, "tensor", Z_HI)
    small_z = send_z(small, 2)
    in_2, share_dproj, out_1, kept, sent, small, small_z = together(
        in_2, share_dproj, out_1, kept, sent, small, small_z
    )

    in_3, in_1 = to_z_cols(share_dproj, 3), to_z_cols(share_dproj, 1)
    kept = bf16(kept + f32(sent)).reshape(half, 2, blk)
    at = core ^ z % 2
    theirs = swap_core(lax.dynamic_index_in_dim(kept, 1 - at, 1, keepdims=False))
    mixed = jnp.concatenate([lax.dynamic_index_in_dim(kept, at, 1, keepdims=False), theirs], 0)
    mixed = lax.ppermute(half_first(mixed), ("dp", "tensor"), TRANSPOSED)
    small = small + small_z
    for step in (1, 2):
        small = small + send_x(small, step)

    grad_out = total(slot(share_out, 0, blk), [out_1, out_2, out_3])
    grad_in = total(col_slot(share_dproj, 0, blk), [in_1, in_2, in_3]).T
    heads = a_log.shape[0]
    return (
        mixed,
        grad_in,
        grad_out,
        small[:heads],
        small[heads : 2 * heads],
        small[2 * heads : 3 * heads],
        small[3 * heads :],
    )


def solution(mesh):
    return jax.shard_map(
        per_device,
        mesh=mesh,
        in_specs=(
            P("dp", None),
            P("dp", "tensor"),
            P("dp", "tensor"),
            P("tensor"),
            P("tensor"),
            P("tensor"),
            P("tensor"),
            P("dp", None),
        ),
        out_specs=(
            P("dp", "tensor"),
            P("dp", "tensor"),
            P("dp", "tensor"),
            P("tensor"),
            P("tensor"),
            P("tensor"),
            P("tensor"),
        ),
        check_vma=False,
    )
```

```python
import jax
import jax.numpy as jnp
from jax import lax
from jax.sharding import PartitionSpec as P

HEAD_DIM = 64
N_STATE = 128
N_X = 4
N_Z = 4

eps = 1e-05

CORE = [(i, i ^ 1) for i in range(16)]
Z_HI = [(i, i ^ 2) for i in range(16)]


def mixer_part(projected, partner_bc, a_log, dt_bias, d_skip, lower_half):
    heads = a_log.shape[0]
    inner_width = heads * HEAD_DIM
    half_state = partner_bc.shape[1] // 2
    seq_len = projected.shape[0]
    inputs = projected[:, :inner_width].reshape(seq_len, heads, HEAD_DIM)
    base = inner_width
    own_b = projected[:, base : base + half_state]
    own_c = projected[:, base + half_state : base + 2 * half_state]
    step_raw = projected[:, base + 2 * half_state :]
    other_b = partner_bc[:, :half_state]
    other_c = partner_bc[:, half_state:]
    full_b = jnp.where(
        lower_half, jnp.concatenate([own_b, other_b], 1), jnp.concatenate([other_b, own_b], 1)
    )
    full_c = jnp.where(
        lower_half, jnp.concatenate([own_c, other_c], 1), jnp.concatenate([other_c, own_c], 1)
    )
    step_size = jax.nn.softplus(step_raw + dt_bias)
    before_or_at = jnp.arange(seq_len)[:, None] >= jnp.arange(seq_len)[None, :]
    log_decay = jnp.dot(
        before_or_at.astype(jnp.float32),
        step_size * -jnp.exp(a_log),
        precision=lax.Precision.HIGHEST,
    )
    causal = before_or_at[:, :, None]
    log_ratio = log_decay[:, None, :] - log_decay[None, :, :]
    decay = jnp.where(causal, jnp.exp(jnp.where(causal, log_ratio, 0.0)), 0.0)
    affinity = jnp.dot(
        full_c.astype(jnp.bfloat16),
        full_b.T.astype(jnp.bfloat16),
        preferred_element_type=jnp.float32,
    )
    weights_ts = decay * affinity[:, :, None] * step_size[None, :, :]
    outputs = jnp.einsum("tsh,shp->thp", weights_ts, inputs, precision=lax.Precision.HIGHEST)
    outputs = outputs + d_skip[None, :, None] * inputs
    return outputs.reshape(seq_len, inner_width)


def gate_part(outputs, gate):
    gated = outputs * jax.nn.silu(gate)
    return (gated, jnp.sum(gated * gated, axis=1))


def together(*values):
    return lax.optimization_barrier(values)


def send_x(block, step):
    return lax.ppermute(block, "dp", [(i, i ^ step * N_Z) for i in range(16)])


def send_z(block, step):
    return lax.ppermute(block, "dp", [(i, i ^ step) for i in range(16)])


def send_turned(block, step):
    route = []
    for x in range(4):
        for z in range(4):
            for y in range(4):
                for r in range(4):
                    source = (x * 4 + z) * 16 + y * 4 + r
                    route.append((source, ((y ^ step) * 4 + z) * 16 + x * 4 + r))
    return lax.ppermute(block, ("dp", "tensor"), route)


def swap_core(block):
    return lax.ppermute(block, "tensor", CORE)


def f32(a):
    return a.astype(jnp.float32)


def bf16(a):
    return a.astype(jnp.bfloat16)


def per_device(tokens, in_weight, out_weight, a_log, dt_bias, d_skip, norm_gain, d_mixed):
    inner_width = norm_gain.shape[0]
    seq_len = tokens.shape[0]
    half = seq_len // 2
    blk = in_weight.shape[0]
    wide = N_Z * blk
    dp = lax.axis_index("dp")
    tensor = lax.axis_index("tensor")
    x, z = dp // N_Z, dp % N_Z
    y, z_hi, core = tensor // 4, tensor // 2 % 2, tensor % 2
    lower_half = core == 0
    mine, other = core * half, half - core * half


    def dot(a, b, dims):
        return lax.dot_general(a, b, (dims, ((), ())), preferred_element_type=jnp.float32)

    def half_first(a):
        return jnp.where(lower_half, a, jnp.concatenate([a[half:], a[:half]], 0))

    def slab(a, shift, start):
        return lax.dynamic_slice(a, (start, (x ^ shift) * wide), (half, wide))

    def grouped(a, received):
        rows = [slab(a, 0, mine), slab(a, 0, other)]
        for r in received:
            rows += r
        return lax.optimization_barrier(jnp.concatenate(rows, 0))

    def by_slot(a):
        columns = [lax.dynamic_slice(a, (0, (z ^ s) * blk), (a.shape[0], blk)) for s in range(N_Z)]
        return lax.optimization_barrier(jnp.concatenate(columns, 1))

    def rows_of(own, received):
        return lax.optimization_barrier(jnp.concatenate([own, *received], 0))

    def slot(a, s, size):
        return a[s * size : (s + 1) * size]

    def cols_of(own, received):
        return lax.optimization_barrier(jnp.concatenate([own, *received], 1))

    def col_slot(a, s, size):
        return a[:, s * size : (s + 1) * size]

    def gather_x(block):
        return [send_x(block, s) for s in (1, 2, 3)]

    def to_z(share, step):
        return send_z(slot(share, step, blk), step)

    def to_z_cols(share, step):
        return send_z(col_slot(share, step, blk), step)

    def total(own, received):
        return f32(own) + sum(f32(r) for r in received)

    in_t = in_weight.T
    in_2, in_1 = send_z(in_t, 2), send_z(in_t, 1)
    tok_in = [send_x(slab(tokens, s, mine), s) for s in (1, 2, 3)]
    in_t, in_2, in_1, tok_in = together(in_t, in_2, in_1, tok_in)

    in_3 = send_z(in_t, 3)
    cot_in = [send_x(slab(d_mixed, s, mine), s) for s in (1, 2, 3)]
    tok = by_slot(grouped(tokens, [(r, swap_core(r)) for r in tok_in]))
    in_3, cot_in, tok, own_out = together(in_3, cot_in, tok, out_weight)

    share_in = bf16(dot(cols_of(in_t, [in_1, in_2, in_3]), tok, ((1,), (1,))))
    proj_in = [send_x(col_slot(share_in, s, seq_len), s) for s in (1, 2, 3)]
    out_2, out_3, out_1 = [send_z(own_out, s) for s in (2, 3, 1)]
    cot = by_slot(grouped(d_mixed, [(r, swap_core(r)) for r in cot_in]))
    proj_in, out_1, out_2, out_3, own_out, cot = together(
        proj_in, out_1, out_2, out_3, own_out, cot
    )

    w_out = rows_of(own_out, [out_1, out_2, out_3])
    share_cot = bf16(dot(cot, w_out, ((1,), (0,))))
    cot_sums = [send_x(slot(share_cot, s, seq_len), s) for s in (1, 2, 3)]
    projected = half_first(bf16(total(col_slot(share_in, 0, seq_len), proj_in)).T)
    proj_gate = projected[:, :inner_width]
    proj_scan = projected[:, inner_width:]
    own_bc = proj_scan[:, inner_width : inner_width + N_STATE]
    partner_bc = swap_core(own_bc)

    def section_scan(proj_vals, partner_vals, rates, biases, skips):
        return mixer_part(proj_vals, partner_vals, rates, biases, skips, lower_half)

    outputs, pull_scan = jax.vjp(
        section_scan, f32(proj_scan), f32(partner_bc), a_log, dt_bias, d_skip
    )
    (gated, squares), pull_gate = jax.vjp(gate_part, outputs, f32(proj_gate))
    total_sq = squares + swap_core(squares)

    def section_norm(gated_vals, sums, gains):
        return gated_vals * lax.rsqrt(sums / (2 * inner_width) + eps)[:, None] * gains

    normed_f32, pull_norm = jax.vjp(section_norm, gated, total_sq, norm_gain)
    own_normed = half_first(bf16(normed_f32))
    normed_in = gather_x(own_normed)
    cot_sums, normed_in = together(cot_sums, normed_in)

    d_normed = half_first(total(slot(share_cot, 0, seq_len), cot_sums))
    d_gated, d_total, d_gain = pull_norm(d_normed)
    d_squares = d_total + swap_core(d_total)
    d_outputs, d_gate = pull_gate((d_gated, d_squares))
    d_scan, d_partner, d_rates, d_biases, d_skips = pull_scan(d_outputs)
    returned = swap_core(bf16(d_partner))
    d_proj = jnp.concatenate(
        [
            d_gate,
            d_scan[:, :inner_width],
            d_scan[:, inner_width : inner_width + N_STATE] + f32(returned),
            d_scan[:, inner_width + N_STATE :],
        ],
        1,
    )
    own_proj = half_first(bf16(d_proj)).T
    small = jnp.concatenate([d_rates, d_biases, d_skips, d_gain])
    own_proj, small, normed_in = together(own_proj, small, normed_in)

    dproj_in = gather_x(own_proj)
    normed = rows_of(own_normed, normed_in)
    share_out = bf16(dot(cot, normed, ((0,), (0,))))
    out_2, out_3 = to_z(share_out, 2), to_z(share_out, 3)
    shares = bf16(dot(normed, w_out, ((1,), (1,))))

    for step in (1, 2):
        small = small + send_z(small, step)
    def halves(first):
        return jnp.concatenate(
            [shares[s * seq_len + first : s * seq_len + first + half] for s in range(N_X)], 0
        )

    own_half, passed = halves(0), halves(half)
    out_2, share_out = together(out_2, share_out)
    out_1 = to_z(share_out, 1)
    dproj_in, out_1, out_3, own_half, passed, small = together(
        dproj_in, out_1, out_3, own_half, passed, small
    )

    share_dproj = bf16(dot(cols_of(own_proj, dproj_in), tok, ((1,), (0,))))
    passed, share_dproj = together(passed, share_dproj)
    chip = bf16(f32(own_half) + f32(swap_core(passed)))
    in_2 = to_z_cols(share_dproj, 2)
    def piece(step):
        return lax.dynamic_slice(chip, ((x ^ y ^ step) * half, 0), (half, wide))

    turned = [send_turned(piece(step), step) for step in range(4)]
    in_2, share_dproj, turned = together(in_2, share_dproj, turned)

    in_3, in_1 = to_z_cols(share_dproj, 3), to_z_cols(share_dproj, 1)
    for step in (1, 2):
        small = small + send_x(small, step)
    summed = sum(f32(r) for r in turned)
    keep = z_hi ^ z // 2
    sent = bf16(lax.dynamic_slice(summed, (0, (1 - keep) * 2 * blk), (half, 2 * blk)))
    kept = lax.dynamic_slice(summed, (0, keep * 2 * blk), (half, 2 * blk))
    kept = bf16(kept + f32(lax.ppermute(sent, "tensor", Z_HI)))
    at = core ^ z % 2
    theirs = swap_core(lax.dynamic_slice(kept, (0, (1 - at) * blk), (half, blk)))
    mixed = jnp.concatenate([lax.dynamic_slice(kept, (0, at * blk), (half, blk)), theirs], 0)
    mixed = half_first(mixed)

    grad_out = total(slot(share_out, 0, blk), [out_1, out_2, out_3])
    grad_in = total(col_slot(share_dproj, 0, blk), [in_1, in_2, in_3]).T
    heads = a_log.shape[0]
    return (
        mixed,
        grad_in,
        grad_out,
        small[:heads],
        small[heads : 2 * heads],
        small[2 * heads : 3 * heads],
        small[3 * heads :],
    )


def solution(mesh):
    return jax.shard_map(
        per_device,
        mesh=mesh,
        in_specs=(
            P("dp", None),
            P("dp", "tensor"),
            P("dp", "tensor"),
            P("tensor"),
            P("tensor"),
            P("tensor"),
            P("tensor"),
            P("dp", None),
        ),
        out_specs=(
            P("dp", "tensor"),
            P("dp", "tensor"),
            P("dp", "tensor"),
            P("tensor"),
            P("tensor"),
            P("tensor"),
            P("tensor"),
        ),
        check_vma=False,
    )
```
